128 devices in a mesh: prow: 4 (over z), pcol: 32 (over x, y, core).
Axes of the slice: x: 4, y: 4, z: 4, core: 2. Of those that a mesh axis runs over, the one named last changes fastest.
Arguments:
- right_side: float32 [4, 32, 256, 128], P('prow', 'pcol'), may hold values from -6 to 6
- factor_tiles: bfloat16 [4, 32, 128, 256, 256], P(None, 'pcol', 'prow'), may hold values from -0.03125 to 0.03125
- tile_scales: float32 [4, 32, 128], P(None, 'pcol', 'prow'), may hold values from 0.25 to 4
- tile_pattern: int32 [4, 32, 128], P(None, 'pcol', 'prow'), may hold values from 0 to 1, as said below
- parent: int32 [128], replicated, may hold values from 0 to 128, as said below
- inverses: bfloat16 [2, 4, 32, 256, 256], P(None, 'prow', 'pcol'), may hold values from -3 to 3
Outputs:
- forward: float32 [4, 32, 256, 128], P('prow', 'pcol')
- solution: float32 [4, 32, 256, 128], P('prow', 'pcol')
The draws below stay inside these ranges and needn't reach their ends.
Inputs may be any that keep to these rules, and one draw needn't show every extreme that they name: A panel of depth d > 0 has as parent a panel of depth d - 1; roots have parent 128; every depth from 0 to 3 occurs. `tile_pattern`: tile_pattern_ij is 1 only where panel i is an ancestor of panel j or panel j an ancestor of panel i in the tree given by parent.
All inputs are finite; a program needn't handle non-finite values.
Results may differ from the reference program's by a relative error of at most 0.0023.
Values may be sent and summed in bfloat16 or wider, within the bound.
No kernel may reach another device: no remote copies, remote signals or barrier semaphores. Data moves between devices by JAX's collectives and lax.ppermute only.
A program may use at most 64 MiB of HBM per device.

```python
import math
import jax
import jax.numpy as jnp
from jax import lax

B = 256
R = 128
DEPTH = 4
GRID_ROWS = 4
GRID_COLS = 32
NB = 128


def build_tree(key):
    key = jax.random.fold_in(key, 9)
    first_key, second_key, third_key = jax.random.split(key, 3)
    ticket = jax.random.randint(first_key, (NB,), 1, 2 ** DEPTH).astype(jnp.int32)
    levels = jnp.zeros((NB,), jnp.int32)
    for power in range(1, DEPTH):
        levels = levels + (ticket >= 2 ** power).astype(jnp.int32)
    shuffled = jax.random.permutation(second_key, NB).astype(jnp.int32)
    position = jnp.zeros((NB,), jnp.int32).at[shuffled].set(jnp.arange(NB, dtype=jnp.int32))
    levels = jnp.where(position < DEPTH, position, levels).astype(jnp.int32)
    scores = jax.random.randint(third_key, (NB, NB), 0, NB).astype(jnp.int32) * NB + jnp.arange(NB, dtype=jnp.int32)[None, :]
    eligible = levels[None, :] == levels[:, None] - 1
    chosen = jnp.argmax(jnp.where(eligible, scores, -1), axis=1).astype(jnp.int32)
    return jnp.where(levels > 0, chosen, NB).astype(jnp.int32)


def draw_parent(key, part):
    return build_tree(key)


def draw_tile_pattern(key, part):
    parent = build_tree(key)
    key = jax.random.fold_in(key, 13)
    extended = jnp.concatenate([parent, jnp.full((1,), NB, jnp.int32)])
    columns = jnp.arange(NB + 1, dtype=jnp.int32)[None, :]
    above = jnp.zeros((NB, NB + 1), jnp.int32)
    current = parent
    for repeat in range(DEPTH - 1):
        above = jnp.maximum(above, (current[:, None] == columns).astype(jnp.int32))
        current = extended[current]
    ancestor = above[:, :NB]
    related = jnp.maximum(ancestor, ancestor.T)
    fill = jax.random.randint(key, (NB, NB), 0, 4).astype(jnp.int32)
    pattern = related * (fill < 3).astype(jnp.int32)
    return pattern.reshape(GRID_ROWS, GRID_COLS, NB).astype(jnp.int32)


def draw_inverses(key, part):
    key = jax.random.fold_in(key, 5)
    first_key, second_key = jax.random.split(key)
    rows_idx = jnp.arange(B)[:, None]
    cols_idx = jnp.arange(B)[None, :]
    identity_mat = (rows_idx == cols_idx).astype(jnp.float32)
    diagonal = jnp.exp(jax.random.uniform(first_key, (2, GRID_ROWS, GRID_COLS, B, 1), jnp.float32, jnp.log(0.5), jnp.log(2.0)))
    spread_part = jax.random.normal(second_key, (2, GRID_ROWS, GRID_COLS, B, B), jnp.float32) * (0.5 / B ** 0.5)
    return (identity_mat * diagonal + spread_part).astype(jnp.bfloat16)


def shard_levels(rng, dims, pieces, low, largest):
    def one(axis_at, parts):
        steps = jax.random.uniform(jax.random.fold_in(jax.random.fold_in(rng, 6), axis_at), (parts,), jnp.float32, low / len(pieces), largest / len(pieces))
        return jnp.repeat(jnp.exp(steps), dims[axis_at] // parts).reshape((-1,) + (1,) * (len(dims) - axis_at - 1))

    loudness = one(*pieces[0])
    for cut in pieces[1:]:
        loudness = loudness * one(*cut)
    return loudness


def gaussian(stream_key, extent, scale, bound, pieces=(), kind=jnp.bfloat16):
    array = jax.random.normal(stream_key, extent, jnp.float32) * scale
    if len(pieces) > 0:
        array = shard_levels(stream_key, extent, pieces, -0.22, 0.18) * array
    return jnp.clip(array, min=-bound, max=bound).astype(kind)


def setup_inputs(seed: int = 0) -> dict:
    splits = jax.random.split(jax.random.key(seed), 7)
    right_side = gaussian(splits[0], (GRID_ROWS, GRID_COLS, B, R), 1.0, 6.0, ((0, 4), (1, 32)), jnp.float32)
    factor_tiles = gaussian(splits[1], (GRID_ROWS, GRID_COLS, NB, B, B), (B * NB) ** -0.5, 0.03125, ((1, 32), (2, 4)))
    tile_scales = jnp.clip(jnp.exp(math.log(4.0) - 2.7725887 * jax.random.uniform(splits[2], (GRID_ROWS, GRID_COLS, NB), jnp.float32) ** shard_levels(splits[2], (GRID_ROWS, GRID_COLS, NB), ((1, 32), (2, 4)), -0.2, 0.2)), 0.25, 4.0)
    tile_pattern = draw_tile_pattern(jax.random.fold_in(splits[6], 71), 0)
    parent = draw_parent(jax.random.fold_in(splits[6], 71), 0)
    inverses = draw_inverses(jax.random.fold_in(splits[6], 71), 0)
    return dict(right_side=right_side, factor_tiles=factor_tiles, tile_scales=tile_scales, tile_pattern=tile_pattern, parent=parent, inverses=inverses)


def depth_table(parent):
    depths = jnp.zeros((NB,), jnp.int32)
    for repeat in range(DEPTH - 1):
        extended = jnp.concatenate([depths, jnp.full((1,), -1, jnp.int32)])
        depths = (extended[parent] + 1).astype(jnp.int32)
    return depths


def apply_inverse(inverse_all, vectors):
    return jnp.einsum("ikl,ilr->ikr", inverse_all, vectors, precision=lax.Precision.HIGHEST)


def refine(target, inverse_all, weights, panels, solved):
    rounded = lax.optimization_barrier(solved.astype(jnp.bfloat16)).astype(jnp.float32)

    def one_row(paired):
        tile_row, weight_row = paired
        product = jnp.einsum("jkl,jlr->jkr", tile_row.astype(jnp.float32), rounded)
        return jnp.sum(weight_row[:, None, None] * product, axis=0)

    partial_rows = lax.map(one_row, (panels, weights))
    return apply_inverse(inverse_all, target - partial_rows)


def reference(right_side, factor_tiles, tile_scales, tile_pattern, parent, inverses):
    target = right_side.reshape(NB, B, R)
    panels = factor_tiles.reshape(NB, NB, B, B)
    kept_weight = tile_scales.reshape(NB, NB) * (tile_pattern.reshape(NB, NB) == 1).astype(jnp.float32)
    depths = depth_table(parent)
    lower_weight = kept_weight * (depths[None, :] > depths[:, None]).astype(jnp.float32)
    upper_weight = kept_weight * (depths[None, :] < depths[:, None]).astype(jnp.float32)
    inverse_all = inverses.reshape(2, NB, B, B).astype(jnp.float32)
    forward = apply_inverse(inverse_all[0], target)
    for repeat in range(DEPTH - 1):
        forward = refine(target, inverse_all[0], lower_weight, panels, forward)
    solution = apply_inverse(inverse_all[1], forward)
    for repeat in range(DEPTH - 1):
        solution = refine(forward, inverse_all[1], upper_weight, panels, solution)
    return forward.reshape(GRID_ROWS, GRID_COLS, B, R), solution.reshape(GRID_ROWS, GRID_COLS, B, R)
```

```python
import functools
import jax
import jax.numpy as jnp
from jax import lax
from jax.experimental import pallas as pl
from jax.experimental.pallas import tpu as pltpu
from jax.sharding import PartitionSpec as P

DEPTH = 4
B = 256
R = 128
SLOTS = 8
SHIFTS = (0, 1, 3, 2)
ANY = pl.BlockSpec(memory_space=pl.ANY)
SMEM = pl.BlockSpec(memory_space=pltpu.SMEM)
VMEM = pl.BlockSpec(memory_space=pltpu.VMEM)


def y_pairs(k):
    return [(i, (i & 25) | ((((i >> 1) + k) & 3) << 1)) for i in range(32)]


def x_pairs(k):
    return [(i, (i & 7) | ((((i >> 3) + k) & 3) << 3)) for i in range(32)]


def z_pairs(k):
    return [(i, (i + k) & 3) for i in range(4)]


CORE_PAIRS = [(i, i ^ 1) for i in range(32)]


def depth_table(parent, levels_count):
    number = parent.shape[0]
    matches = parent[:, None] == jnp.arange(number, dtype=jnp.int32)[None, :]
    depths = jnp.zeros((number,), jnp.int32)
    for repeat in range(levels_count - 1):
        depths = jnp.sum(jnp.where(matches, depths[None, :] + 1, 0), axis=1)
    return depths


def work_lists(depth_rows, depth_cols, pattern):
    row_depth = depth_rows[:, None]
    col_depth = depth_cols[None, :]
    step = jnp.where(col_depth > row_depth, 3 - col_depth, jnp.where(col_depth < row_depth, 3 + col_depth, 6))
    step = jnp.where(pattern == 1, step, 6).reshape(-1)
    number = jnp.arange(128, dtype=jnp.int32)
    before = (step[None, :] < step[:, None]) | ((step[None, :] == step[:, None]) & (number[None, :] < number[:, None]))
    place = jnp.sum(before.astype(jnp.int32), axis=1)
    order = jnp.sum(jnp.where(place[None, :] == number[:, None], number[None, :], 0), axis=1)
    starts = jnp.sum((step[None, :] < jnp.arange(8, dtype=jnp.int32)[:, None]).astype(jnp.int32), axis=1)
    return order, starts


def tile_kernel(step, order, starts, scales, place, *refs):
    pieces = refs[:8]
    tiles = refs[8]
    outs = refs[9:13]
    acc, tile_buf, panel_buf, tile_sem, panel_sem = refs[13:]
    first, last = starts[step], starts[step + 1]
    prow_at, pcol_at = place[0], place[1]

    def copies(n, slot, act):
        code = order[n]
        row, col = code // 32, code % 32
        act(pltpu.make_async_copy(tiles.at[row, col], tile_buf.at[slot], tile_sem.at[slot]))
        other = (col ^ pcol_at) & 1
        x_back = ((pcol_at >> 3) - (col >> 3)) & 3
        y_back = (((pcol_at >> 1) & 3) - ((col >> 1) & 3)) & 3
        y_slot = jnp.where(y_back == 2, 3, jnp.where(y_back == 3, 2, y_back))
        return other, x_back, y_slot

    def start(n, slot):
        other, x_back, y_slot = copies(n, slot, lambda c: c.start())
        for e in range(2):
            for k in range(4):
                @pl.when((other == e) & (x_back == SHIFTS[k]))
                def _():
                    pltpu.make_async_copy(pieces[e * 4 + k].at[y_slot], panel_buf.at[slot], panel_sem.at[slot]).start()

    for n in range(SLOTS):
        @pl.when(first + n < last)
        def _():
            start(first + n, n)

    acc[...] = jnp.zeros_like(acc)

    def body(n, carry):
        slot = (n - first) % SLOTS
        code = order[n]
        pltpu.make_async_copy(tiles.at[0, 0], tile_buf.at[slot], tile_sem.at[slot]).wait()
        pltpu.make_async_copy(pieces[0].at[0], panel_buf.at[slot], panel_sem.at[slot]).wait()
        product = jnp.dot(tile_buf[slot], panel_buf[slot], preferred_element_type=jnp.float32)
        row = code // 32
        acc[row] = acc[row] + scales[code] * product

        @pl.when(n + SLOTS < last)
        def _():
            start(n + SLOTS, slot)
        return carry

    lax.fori_loop(first, last, body, 0)
    outs[0][...] = acc[prow_at]
    for k in range(1, 4):
        outs[k][...] = acc[(prow_at + SHIFTS[k]) & 3].astype(jnp.bfloat16)


def tile_products(step, order, starts, scales, place, pieces, tiles):
    return pl.pallas_call(
        functools.partial(tile_kernel, step),
        out_shape=[jax.ShapeDtypeStruct((B, R), jnp.float32)] + [jax.ShapeDtypeStruct((B, R), jnp.bfloat16)] * 3,
        in_specs=[SMEM] * 4 + [ANY] * 9,
        out_specs=[VMEM] * 4,
        scratch_shapes=[
            pltpu.VMEM((4, B, R), jnp.float32),
            pltpu.VMEM((SLOTS, B, B), jnp.bfloat16),
            pltpu.VMEM((SLOTS, B, R), jnp.bfloat16),
            pltpu.SemaphoreType.DMA((SLOTS,)),
            pltpu.SemaphoreType.DMA((SLOTS,)),
        ],
        compiler_params=pltpu.CompilerParams(vmem_limit_bytes=50 * 2**20),
        cost_estimate=pl.CostEstimate(flops=2 * 4 * B * B * R, bytes_accessed=4 * (B * B + B * R) * 2, transcendentals=0),
        name="tile_products",
    )(order, starts, scales, place, *pieces, tiles)


def apply_inverse(inverse, vectors):
    high = vectors.astype(jnp.bfloat16)
    low = (vectors - high.astype(jnp.float32)).astype(jnp.bfloat16)
    return jnp.dot(inverse, high, preferred_element_type=jnp.float32) + jnp.dot(inverse, low, preferred_element_type=jnp.float32)


def first_kernel(target, inverse, solved, rounded):
    value = apply_inverse(inverse[...], target[...])
    solved[...] = value
    rounded[...] = value.astype(jnp.bfloat16)


def first_solve(target, inverse):
    return pl.pallas_call(
        first_kernel,
        out_shape=[jax.ShapeDtypeStruct((B, R), jnp.float32), jax.ShapeDtypeStruct((B, R), jnp.bfloat16)],
        in_specs=[VMEM] * 2,
        out_specs=[VMEM] * 2,
        cost_estimate=pl.CostEstimate(flops=4 * B * B * R, bytes_accessed=B * R * 12, transcendentals=0),
        name="first_solve",
    )(target, inverse)


def next_kernel(target, inverse, total, own, one, two, three, new_total, solved, rounded):
    summed = total[...] + own[...] + (one[...].astype(jnp.float32) + two[...].astype(jnp.float32) + three[...].astype(jnp.float32))
    new_total[...] = summed
    value = apply_inverse(inverse[...], target[...] - summed)
    solved[...] = value
    rounded[...] = value.astype(jnp.bfloat16)


def next_solve(target, inverse, total, parts):
    return pl.pallas_call(
        next_kernel,
        out_shape=[jax.ShapeDtypeStruct((B, R), jnp.float32)] * 2 + [jax.ShapeDtypeStruct((B, R), jnp.bfloat16)],
        in_specs=[VMEM] * 7,
        out_specs=[VMEM] * 3,
        cost_estimate=pl.CostEstimate(flops=4 * B * B * R, bytes_accessed=B * R * 20, transcendentals=0),
        name="next_solve",
    )(target, inverse, total, *parts)


def gather_panels(panel):
    along_y = [panel] + [lax.ppermute(panel, "pcol", y_pairs(k)) for k in SHIFTS[1:]]
    stacked = jnp.stack(along_y)
    along_x = [stacked] + [lax.ppermute(stacked, "pcol", x_pairs(k)) for k in SHIFTS[1:]]
    return along_x + [lax.ppermute(piece, "pcol", CORE_PAIRS) for piece in along_x]


def shards(right_side, factor_tiles, tile_scales, tile_pattern, parent, inverses):
    prow_at = lax.axis_index("prow")
    pcol_at = lax.axis_index("pcol")
    depths = depth_table(parent, DEPTH)
    depth_rows = lax.dynamic_index_in_dim(depths.reshape(4, 32), pcol_at, 1, keepdims=False)
    depth_cols = lax.dynamic_slice_in_dim(depths, prow_at * 32, 32)
    order, starts = work_lists(depth_rows, depth_cols, tile_pattern[:, 0])
    scales = tile_scales.reshape(-1)
    place = jnp.stack([prow_at, pcol_at]).astype(jnp.int32)
    tiles = factor_tiles[:, 0]

    def sweep(target, inverse, first_step):
        solved, rounded = first_solve(target, inverse)
        total = jnp.zeros_like(target)
        for step in range(first_step, first_step + DEPTH - 1):
            pieces = gather_panels(rounded)
            parts = tile_products(step, order, starts, scales, place, pieces, tiles)
            received = [parts[0]] + [lax.ppermute(parts[k], "prow", z_pairs(SHIFTS[k])) for k in (1, 2, 3)]
            total, solved, rounded = next_solve(target, inverse, total, received)
        return solved

    forward = sweep(right_side[0, 0], inverses[0, 0, 0], 0)
    solution = sweep(forward, inverses[1, 0, 0], 3)
    return (forward[None, None], solution[None, None])


def solution(mesh):
    in_specs = (
        P("prow", "pcol", None, None),
        P(None, "pcol", "prow", None, None),
        P(None, "pcol", "prow"),
        P(None, "pcol", "prow"),
        P(),
        P(None, "prow", "pcol", None, None),
    )
    out_specs = (P("prow", "pcol", None, None), P("prow", "pcol", None, None))
    return jax.shard_map(shards, mesh=mesh, in_specs=in_specs, out_specs=out_specs, check_vma=False)
```

```python
import functools
import jax
import jax.numpy as jnp
from jax import lax
from jax.experimental import pallas as pl
from jax.experimental.pallas import tpu as pltpu
from jax.sharding import PartitionSpec as P

DEPTH = 4
B = 256
R = 128
SLOTS = 8
SHIFTS = (0, 1, 3, 2)
ANY = pl.BlockSpec(memory_space=pl.ANY)
SMEM = pl.BlockSpec(memory_space=pltpu.SMEM)
VMEM = pl.BlockSpec(memory_space=pltpu.VMEM)
HBM = pl.BlockSpec(memory_space=pltpu.HBM)
LIMIT = 50 * 2**20
READY = 24


def near_pairs(k):
    return [(i, shifted(i, k, 1 if i & 1 == 0 else 3)) for i in range(32)]


def far_pairs(k):
    return [(i, shifted(i, k, 3 if i & 1 == 0 else 1)) for i in range(32)]


def shifted(i, k, bit):
    return (i & ~(3 << bit)) | ((((i >> bit) + k) & 3) << bit)


def z_pairs(k):
    return [(i, (i + k) & 3) for i in range(4)]


CORE_PAIRS = [(i, i ^ 1) for i in range(32)]


def plan_kernel(place, parent, pattern, out):
    prow_at, pcol_at = place[0], place[1]
    down = lax.broadcasted_iota(jnp.int32, (128, 128), 0)
    across = lax.broadcasted_iota(jnp.int32, (128, 128), 1)

    def column(row):
        return jnp.broadcast_to(row, (128, 128)).T

    def total(values):
        return jnp.sum(values, axis=0, keepdims=True)

    matches = parent[...] == down
    depths = jnp.zeros((1, 128), jnp.int32)
    for repeat in range(DEPTH - 1):
        depths = total(jnp.where(matches, column(depths) + 1, 0))
    depth_column = column(depths)
    row_depth = total(jnp.where(down == (across & 96) + pcol_at, depth_column, 0))
    col_depth = total(jnp.where(down == (across & 31) + prow_at * 32, depth_column, 0))
    spread = (lax.broadcasted_iota(jnp.int32, (32, 128), 1) & 31) == lax.broadcasted_iota(jnp.int32, (32, 128), 0)
    kept = jnp.zeros((1, 128), jnp.float32)
    for row in range(4):
        ones = (jnp.broadcast_to(pattern[row], (8, 32)) == 1).astype(jnp.float32)
        wide = jnp.dot(ones, spread.astype(jnp.float32), preferred_element_type=jnp.float32)[:1]
        kept = jnp.where(across[:1] >> 5 == row, wide, kept)
    step = jnp.where(col_depth > row_depth, 3 - col_depth, jnp.where(col_depth < row_depth, 3 + col_depth, 6))
    step = jnp.where(kept > 0.5, step, 6)
    steps = column(step)
    before = (steps < step) | ((steps == step) & (down < across))
    places = total(before.astype(jnp.int32))
    out[0:1] = total(jnp.where(column(places) == across, down, 0))
    out[1:2] = total((steps < across).astype(jnp.int32))


def make_plan(place, parent, pattern):
    return pl.pallas_call(
        plan_kernel,
        out_shape=jax.ShapeDtypeStruct((2, 128), jnp.int32),
        in_specs=[SMEM, VMEM, VMEM],
        out_specs=VMEM,
        compiler_params=pltpu.CompilerParams(vmem_limit_bytes=LIMIT),
        cost_estimate=pl.CostEstimate(flops=2**22, bytes_accessed=2**12, transcendentals=0),
        name="make_plan",
    )(place, parent, pattern)


def ready_kernel(plan, tiles, out, sems):
    count = jnp.minimum(plan[1, 6], READY)
    for act in (lambda copy: copy.start(), lambda copy: copy.wait()):
        for n in range(READY):
            @pl.when(n < count)
            def _():
                code = plan[0, n]
                act(pltpu.make_async_copy(tiles.at[code >> 5, code & 31], out.at[n], sems.at[n]))


def ready_tiles(plan, tiles):
    return pl.pallas_call(
        ready_kernel,
        out_shape=jax.ShapeDtypeStruct((READY, B, B), jnp.bfloat16),
        in_specs=[SMEM, ANY],
        out_specs=ANY,
        scratch_shapes=[pltpu.SemaphoreType.DMA((READY,))],
        compiler_params=pltpu.CompilerParams(vmem_limit_bytes=LIMIT),
        cost_estimate=pl.CostEstimate(flops=0, bytes_accessed=2 * READY * B * B * 2, transcendentals=0),
        name="ready_tiles",
    )(plan, tiles)


def fetch(sources, buffers, sems):
    fetched = [pltpu.make_async_copy(src, buf, sems.at[n]) for n, (src, buf) in enumerate(zip(sources, buffers))]
    for copy in fetched:
        copy.start()
    return fetched


def panel_place(pcol_at, col):
    x_back = ((pcol_at >> 3) - (col >> 3)) & 3
    y_back = ((pcol_at >> 1) - (col >> 1)) & 3
    far = jnp.where((col & 1) == 0, x_back, y_back)
    near = jnp.where((col & 1) == 0, y_back, x_back)
    near_slot = jnp.where(near == 2, 3, jnp.where(near == 3, 2, near))
    return (col ^ pcol_at) & 1, far, near_slot


def start_panel(pieces, pcol_at, col, buffer, sem):
    other, far, near_slot = panel_place(pcol_at, col)
    for e in range(2):
        for k in range(4):
            @pl.when((other == e) & (far == SHIFTS[k]))
            def _():
                pltpu.make_async_copy(pieces[e * 4 + k].at[near_slot], buffer, sem).start()


def tile_kernel(step, plan, scales, place, *refs):
    pieces, tiles, ready, refs = refs[:8], refs[8], refs[9], refs[10:]
    before, refs = (refs[0], refs[1:]) if step % 3 > 0 else (None, refs)
    outs, refs = refs[:4], refs[4:]
    after, refs = (refs[0], refs[1:]) if step % 3 < 2 else (None, refs)
    acc, tile_buf, panel_buf, tile_sem, panel_sem, before_sem = refs
    first, last = plan[1, step], plan[1, step + 1]
    prow_at, pcol_at = place[0], place[1]

    def start(n, slot):
        code = plan[0, n]
        row, col = code >> 5, code & 31

        @pl.when(n < READY)
        def _():
            pltpu.make_async_copy(ready.at[n], tile_buf.at[slot], tile_sem.at[slot]).start()

        @pl.when(n >= READY)
        def _():
            pltpu.make_async_copy(tiles.at[row, col], tile_buf.at[slot], tile_sem.at[slot]).start()

        start_panel(pieces, pcol_at, col, panel_buf.at[slot], panel_sem.at[slot])

    if step % 3 > 0:
        previous = pltpu.make_async_copy(before, acc, before_sem)
        previous.start()
    for n in range(SLOTS):
        @pl.when(first + n < last)
        def _():
            start(first + n, n)

    if step % 3 > 0:
        previous.wait()
    else:
        acc[...] = jnp.zeros_like(acc)

    def body(n, carry):
        slot = (n - first) % SLOTS
        code = plan[0, n]
        pltpu.make_async_copy(tiles.at[0, 0], tile_buf.at[slot], tile_sem.at[slot]).wait()
        pltpu.make_async_copy(pieces[0].at[0], panel_buf.at[slot], panel_sem.at[slot]).wait()
        product = jnp.dot(tile_buf[slot], panel_buf[slot], preferred_element_type=jnp.float32)
        row = code >> 5
        acc[row] = acc[row] + scales[row, 0, code & 31] * product

        @pl.when(n + SLOTS < last)
        def _():
            start(n + SLOTS, slot)
        return carry

    lax.fori_loop(first, last, body, 0)
    if after is not None:
        after[...] = acc[...]
    outs[0][...] = acc[prow_at]
    for k in range(1, 4):
        outs[k][...] = acc[(prow_at + SHIFTS[k]) & 3].astype(jnp.bfloat16)


def tile_products(step, plan, scales, place, pieces, tiles, ready, before):
    out_shape = [jax.ShapeDtypeStruct((B, R), jnp.float32)] + [jax.ShapeDtypeStruct((B, R), jnp.bfloat16)] * 3
    if step % 3 < 2:
        out_shape = out_shape + [jax.ShapeDtypeStruct((4, B, R), jnp.float32)]
    return pl.pallas_call(
        functools.partial(tile_kernel, step),
        out_shape=out_shape,
        in_specs=[SMEM] * 3 + [ANY] * (10 + len(before)),
        out_specs=[VMEM] * len(out_shape),
        scratch_shapes=[
            pltpu.VMEM((4, B, R), jnp.float32),
            pltpu.VMEM((SLOTS, B, B), jnp.bfloat16),
            pltpu.VMEM((SLOTS, B, R), jnp.bfloat16),
            pltpu.SemaphoreType.DMA((SLOTS,)),
            pltpu.SemaphoreType.DMA((SLOTS,)),
            pltpu.SemaphoreType.DMA,
        ],
        compiler_params=pltpu.CompilerParams(vmem_limit_bytes=LIMIT),
        cost_estimate=pl.CostEstimate(flops=2 * 4 * B * B * R, bytes_accessed=4 * (B * B + B * R) * 2, transcendentals=0),
        name="tile_products",
    )(plan, scales, place, *pieces, tiles, ready, *before)


def split(vectors):
    high = vectors.astype(jnp.bfloat16)
    return high, (vectors - high.astype(jnp.float32)).astype(jnp.bfloat16)


def apply_split(inverse, high, low):
    return jnp.dot(inverse, high, preferred_element_type=jnp.float32) + jnp.dot(inverse, low, preferred_element_type=jnp.float32)


def solve_kernel(uses, summed, keep, send, target, inverses, *refs):
    sums, refs = refs[:summed], refs[summed:]
    rounded, refs = (refs[0], refs[1:]) if send else (None, refs)
    solved, refs = (refs[0], refs[1:]) if keep else (None, refs)
    buffers, inverse_buf, sems = refs[:-2], refs[-2], refs[-1]
    inverse_copies = fetch([inverses.at[n] for n in uses], [inverse_buf.at[n] for n in range(len(uses))], sems.at[pl.ds(5, 2)])
    for copy in fetch((target,) + sums, buffers, sems):
        copy.wait()
    value = buffers[0][...]
    if sums:
        received = buffers[2][...].astype(jnp.float32) + buffers[3][...].astype(jnp.float32) + buffers[4][...].astype(jnp.float32)
        value = value - (buffers[1][...] + received)
    for n, use in enumerate(uses):
        inverse_copies[n].wait()
        value = apply_split(inverse_buf[n], *split(value))
        if n == 0 and solved is not None:
            solved[...] = value
    if rounded is not None:
        rounded[...] = value.astype(jnp.bfloat16)


def solve(uses, target, inverses, sums, keep=False, send=True):
    out_shape = []
    if send:
        out_shape.append(jax.ShapeDtypeStruct((B, R), jnp.bfloat16))
    if keep:
        out_shape.append(jax.ShapeDtypeStruct((B, R), jnp.float32))
    buffers = [pltpu.VMEM((B, R), jnp.float32)]
    if sums:
        buffers = buffers + [pltpu.VMEM((B, R), jnp.float32)] + [pltpu.VMEM((B, R), jnp.bfloat16)] * 3
    return pl.pallas_call(
        functools.partial(solve_kernel, uses, len(sums), keep, send),
        out_shape=out_shape,
        in_specs=[ANY] * (2 + len(sums)),
        out_specs=[VMEM] * len(out_shape),
        scratch_shapes=buffers + [pltpu.VMEM((len(uses), B, B), jnp.bfloat16), pltpu.SemaphoreType.DMA((7,))],
        compiler_params=pltpu.CompilerParams(vmem_limit_bytes=LIMIT),
        cost_estimate=pl.CostEstimate(flops=4 * B * B * R, bytes_accessed=B * R * 20, transcendentals=0),
        name="solve",
    )(target, inverses, *sums)


def stack_kernel(ready, *refs):
    panels, out, sems = refs[:4], refs[4], refs[5]
    for copy in fetch(panels, [out.at[k] for k in range(4)], sems):
        copy.wait()


def stack_after(ready, panels):
    return pl.pallas_call(
        stack_kernel,
        out_shape=jax.ShapeDtypeStruct((4, B, R), jnp.bfloat16),
        in_specs=[ANY] * 5,
        out_specs=ANY,
        scratch_shapes=[pltpu.SemaphoreType.DMA((4,))],
        compiler_params=pltpu.CompilerParams(vmem_limit_bytes=LIMIT),
        name="stack_after",
    )(ready, *panels)


def gather_panels(panel, ready=None):
    near = [panel] + [lax.ppermute(panel, "pcol", near_pairs(k)) for k in SHIFTS[1:]]
    near = jnp.stack(near) if ready is None else stack_after(ready, near)
    far = [near] + [lax.ppermute(near, "pcol", far_pairs(k)) for k in SHIFTS[1:]]
    return far + [lax.ppermute(piece, "pcol", CORE_PAIRS) for piece in far]


def across_rows(values):
    return [lax.ppermute(value, "prow", z_pairs(k)) for value, k in zip(values, SHIFTS[1:])]


def shards(right_side, factor_tiles, tile_scales, tile_pattern, parent, inverses):
    place = jnp.stack([lax.axis_index("prow"), lax.axis_index("pcol")]).astype(jnp.int32)
    tiles = factor_tiles[:, 0]
    inverse_pair = inverses[:, 0, 0]

    target = right_side[0, 0]
    (rounded,) = solve((0,), target, inverse_pair, ())
    plan = make_plan(place, parent.reshape(1, 128), tile_pattern)
    ready = ready_tiles(plan, tiles)
    before = ()
    for step in range(6):
        pieces = gather_panels(rounded, ready if step == 0 else None)
        parts = tile_products(step, plan, tile_scales, place, pieces, tiles, ready, before)
        before = tuple(parts[4:])
        sums = (parts[0], *across_rows(parts[1:4]))
        if step == 2:
            rounded, forward = solve((0, 1), target, inverse_pair, sums, keep=True)
            target = forward
        elif step == 5:
            (solved,) = solve((1,), target, inverse_pair, sums, keep=True, send=False)
        else:
            (rounded,) = solve((step // 3,), target, inverse_pair, sums)
    return (forward[None, None], solved[None, None])


def solution(mesh):
    in_specs = (
        P("prow", "pcol", None, None),
        P(None, "pcol", "prow", None, None),
        P(None, "pcol", "prow"),
        P(None, "pcol", "prow"),
        P(),
        P(None, "prow", "pcol", None, None),
    )
    out_specs = (P("prow", "pcol", None, None), P("prow", "pcol", None, None))
    return jax.shard_map(shards, mesh=mesh, in_specs=in_specs, out_specs=out_specs, check_vma=False)
```

```python
import functools
import jax
import jax.numpy as jnp
from jax import lax
from jax.experimental import pallas as pl
from jax.experimental.pallas import tpu as pltpu
from jax.sharding import PartitionSpec as P

DEPTH = 4
B = 256
R = 128
SLOTS = 8
NEAR = (0, 3, 1, 2)
FAR = (0, 1, 3, 2)
ACROSS = (0, 2, 1, 3)
ANY = pl.BlockSpec(memory_space=pl.ANY)
SMEM = pl.BlockSpec(memory_space=pltpu.SMEM)
VMEM = pl.BlockSpec(memory_space=pltpu.VMEM)
HBM = pl.BlockSpec(memory_space=pltpu.HBM)
LIMIT = 50 * 2**20


def near_pairs(k):
    return [(i, shifted(i, k, 1 if i & 1 == 0 else 3)) for i in range(32)]


def far_pairs(k):
    return [(i, shifted(i, k, 3 if i & 1 == 0 else 1)) for i in range(32)]


def shifted(i, k, bit):
    return (i & ~(3 << bit)) | ((((i >> bit) + k) & 3) << bit)


def z_pairs(k):
    return [(i, (i + k) & 3) for i in range(4)]


CORE_PAIRS = [(i, i ^ 1) for i in range(32)]


def plan_kernel(place, parent, pattern, out):
    prow_at, pcol_at = place[0], place[1]
    down = lax.broadcasted_iota(jnp.int32, (128, 128), 0)
    across = lax.broadcasted_iota(jnp.int32, (128, 128), 1)

    def column(row):
        return jnp.broadcast_to(row, (128, 128)).T

    def total(values):
        return jnp.sum(values, axis=0, keepdims=True)

    matches = parent[...] == down
    depths = jnp.zeros((1, 128), jnp.int32)
    for repeat in range(DEPTH - 1):
        depths = total(jnp.where(matches, column(depths) + 1, 0))
    depth_column = column(depths)
    row_depth = total(jnp.where(down == (across & 96) + pcol_at, depth_column, 0))
    col_depth = total(jnp.where(down == (across & 31) + prow_at * 32, depth_column, 0))
    spread = (lax.broadcasted_iota(jnp.int32, (32, 128), 1) & 31) == lax.broadcasted_iota(jnp.int32, (32, 128), 0)
    kept = jnp.zeros((1, 128), jnp.float32)
    for row in range(4):
        ones = (jnp.broadcast_to(pattern[row], (8, 32)) == 1).astype(jnp.float32)
        wide = jnp.dot(ones, spread.astype(jnp.float32), preferred_element_type=jnp.float32)[:1]
        kept = jnp.where(across[:1] >> 5 == row, wide, kept)
    step = jnp.where(col_depth > row_depth, 3 - col_depth, jnp.where(col_depth < row_depth, 3 + col_depth, 6))
    step = jnp.where(kept > 0.5, step, 6)
    steps = column(step)
    before = (steps < step) | ((steps == step) & (down < across))
    places = total(before.astype(jnp.int32))
    out[0:1] = total(jnp.where(column(places) == across, down, 0))
    out[1:2] = total((steps < across).astype(jnp.int32))


def make_plan(place, parent, pattern):
    return pl.pallas_call(
        plan_kernel,
        out_shape=jax.ShapeDtypeStruct((2, 128), jnp.int32),
        in_specs=[SMEM, VMEM, VMEM],
        out_specs=VMEM,
        compiler_params=pltpu.CompilerParams(vmem_limit_bytes=LIMIT),
        cost_estimate=pl.CostEstimate(flops=2**22, bytes_accessed=2**12, transcendentals=0),
        name="make_plan",
    )(place, parent, pattern)


def fetch(sources, buffers, sems):
    fetched = [pltpu.make_async_copy(src, buf, sems.at[n]) for n, (src, buf) in enumerate(zip(sources, buffers))]
    for copy in fetched:
        copy.start()
    return fetched


def panel_place(pcol_at, col):
    x_back = ((pcol_at >> 3) - (col >> 3)) & 3
    y_back = ((pcol_at >> 1) - (col >> 1)) & 3
    far = jnp.where((col & 1) == 0, x_back, y_back)
    near = jnp.where((col & 1) == 0, y_back, x_back)
    near_slot = sum(jnp.where(near == shift, n, 0) for n, shift in enumerate(NEAR))
    return (col ^ pcol_at) & 1, far, near_slot


def start_panel(pieces, pcol_at, col, buffer, sem):
    other, far, near_slot = panel_place(pcol_at, col)
    for e in range(2):
        for k in range(4):
            @pl.when((other == e) & (far == FAR[k]))
            def _():
                pltpu.make_async_copy(pieces[e * 4 + k].at[near_slot], buffer, sem).start()


def tile_kernel(step, plan, scales, place, *refs):
    pieces, tiles, refs = refs[:8], refs[8], refs[9:]
    before, refs = (refs[0], refs[1:]) if step % 3 > 0 else (None, refs)
    outs, refs = refs[:4], refs[4:]
    after, refs = (refs[0], refs[1:]) if step % 3 < 2 else (None, refs)
    acc, tile_buf, panel_buf, tile_sem, panel_sem, before_sem = refs
    first, last = plan[1, step], plan[1, step + 1]
    prow_at, pcol_at = place[0], place[1]

    def start(n, slot):
        code = plan[0, n]
        row, col = code >> 5, code & 31

        pltpu.make_async_copy(tiles.at[row, col], tile_buf.at[slot], tile_sem.at[slot]).start()
        start_panel(pieces, pcol_at, col, panel_buf.at[slot], panel_sem.at[slot])

    if step % 3 > 0:
        previous = pltpu.make_async_copy(before, acc, before_sem)
        previous.start()
    def begin(n, carry):
        start(n, n - first)
        return carry

    lax.fori_loop(first, jnp.minimum(last, first + SLOTS), begin, 0)

    if step % 3 > 0:
        previous.wait()
    else:
        acc[...] = jnp.zeros_like(acc)

    def body(n, carry):
        slot = (n - first) % SLOTS
        code = plan[0, n]
        pltpu.make_async_copy(tiles.at[0, 0], tile_buf.at[slot], tile_sem.at[slot]).wait()
        pltpu.make_async_copy(pieces[0].at[0], panel_buf.at[slot], panel_sem.at[slot]).wait()
        product = jnp.dot(tile_buf[slot], panel_buf[slot], preferred_element_type=jnp.float32)
        row = code >> 5
        acc[row] = acc[row] + scales[row, 0, code & 31] * product

        @pl.when(n + SLOTS < last)
        def _():
            start(n + SLOTS, slot)
        return carry

    lax.fori_loop(first, last, body, 0)
    if after is not None:
        after[...] = acc[...]
    outs[0][...] = acc[prow_at]
    for k in range(1, 4):
        outs[k][...] = acc[(prow_at + ACROSS[k]) & 3].astype(jnp.bfloat16)


def tile_products(step, plan, scales, place, pieces, tiles, before):
    out_shape = [jax.ShapeDtypeStruct((B, R), jnp.float32)] + [jax.ShapeDtypeStruct((B, R), jnp.bfloat16)] * 3
    if step % 3 < 2:
        out_shape = out_shape + [jax.ShapeDtypeStruct((4, B, R), jnp.float32)]
    return pl.pallas_call(
        functools.partial(tile_kernel, step),
        out_shape=out_shape,
        in_specs=[SMEM] * 3 + [ANY] * (9 + len(before)),
        out_specs=[VMEM] * len(out_shape),
        scratch_shapes=[
            pltpu.VMEM((4, B, R), jnp.float32),
            pltpu.VMEM((SLOTS, B, B), jnp.bfloat16),
            pltpu.VMEM((SLOTS, B, R), jnp.bfloat16),
            pltpu.SemaphoreType.DMA((SLOTS,)),
            pltpu.SemaphoreType.DMA((SLOTS,)),
            pltpu.SemaphoreType.DMA,
        ],
        compiler_params=pltpu.CompilerParams(vmem_limit_bytes=LIMIT),
        cost_estimate=pl.CostEstimate(flops=2 * 4 * B * B * R, bytes_accessed=4 * (B * B + B * R) * 2, transcendentals=0),
        name="tile_products",
    )(plan, scales, place, *pieces, tiles, *before)


def split(vectors):
    high = vectors.astype(jnp.bfloat16)
    return high, (vectors - high.astype(jnp.float32)).astype(jnp.bfloat16)


def apply_split(inverse, high, low):
    return jnp.dot(inverse, high, preferred_element_type=jnp.float32) + jnp.dot(inverse, low, preferred_element_type=jnp.float32)


def solve_kernel(uses, summed, keep, send, target, inverses, *refs):
    sums, refs = refs[:summed], refs[summed:]
    rounded, refs = (refs[0], refs[1:]) if send else (None, refs)
    solved, refs = (refs[0], refs[1:]) if keep else (None, refs)
    buffers, inverse_buf, sems = refs[:-2], refs[-2], refs[-1]
    inverse_copies = fetch([inverses.at[n] for n in uses], [inverse_buf.at[n] for n in range(len(uses))], sems.at[pl.ds(5, 2)])
    for copy in fetch((target,) + sums, buffers, sems):
        copy.wait()
    value = buffers[0][...]
    if sums:
        received = buffers[2][...].astype(jnp.float32) + buffers[3][...].astype(jnp.float32) + buffers[4][...].astype(jnp.float32)
        value = value - (buffers[1][...] + received)
    for n, use in enumerate(uses):
        inverse_copies[n].wait()
        value = apply_split(inverse_buf[n], *split(value))
        if n == 0 and solved is not None:
            solved[...] = value
    if rounded is not None:
        rounded[...] = value.astype(jnp.bfloat16)


def solve(uses, target, inverses, sums, keep=False, send=True):
    out_shape = []
    if send:
        out_shape.append(jax.ShapeDtypeStruct((B, R), jnp.bfloat16))
    if keep:
        out_shape.append(jax.ShapeDtypeStruct((B, R), jnp.float32))
    buffers = [pltpu.VMEM((B, R), jnp.float32)]
    if sums:
        buffers = buffers + [pltpu.VMEM((B, R), jnp.float32)] + [pltpu.VMEM((B, R), jnp.bfloat16)] * 3
    return pl.pallas_call(
        functools.partial(solve_kernel, uses, len(sums), keep, send),
        out_shape=out_shape,
        in_specs=[ANY] * (2 + len(sums)),
        out_specs=[VMEM] * len(out_shape),
        scratch_shapes=buffers + [pltpu.VMEM((len(uses), B, B), jnp.bfloat16), pltpu.SemaphoreType.DMA((7,))],
        compiler_params=pltpu.CompilerParams(vmem_limit_bytes=LIMIT if sums else 60 * 2**20),
        cost_estimate=pl.CostEstimate(flops=4 * B * B * R, bytes_accessed=B * R * 20, transcendentals=0),
        name="solve",
    )(target, inverses, *sums)


def stack_kernel(plan, *refs):
    panels, out, sems = refs[:4], refs[4], refs[5]
    for copy in fetch(panels, [out.at[k] for k in range(4)], sems):
        copy.wait()


def stack_after(plan, panels):
    return pl.pallas_call(
        stack_kernel,
        out_shape=jax.ShapeDtypeStruct((4, B, R), jnp.bfloat16),
        in_specs=[ANY] * 5,
        out_specs=ANY,
        scratch_shapes=[pltpu.SemaphoreType.DMA((4,))],
        compiler_params=pltpu.CompilerParams(vmem_limit_bytes=LIMIT),
        name="stack_after",
    )(plan, *panels)


def gather_panels(panel, plan=None):
    near = [panel] + [lax.ppermute(panel, "pcol", near_pairs(k)) for k in NEAR[1:]]
    near = jnp.stack(near) if plan is None else stack_after(plan, near)
    far = [near] + [lax.ppermute(near, "pcol", far_pairs(k)) for k in FAR[1:]]
    return far + [lax.ppermute(piece, "pcol", CORE_PAIRS) for piece in far]


def across_rows(values):
    return [lax.ppermute(value, "prow", z_pairs(k)) for value, k in zip(values, ACROSS[1:])]


def shards(right_side, factor_tiles, tile_scales, tile_pattern, parent, inverses):
    place = jnp.stack([lax.axis_index("prow"), lax.axis_index("pcol")]).astype(jnp.int32)
    tiles = factor_tiles[:, 0]
    inverse_pair = inverses[:, 0, 0]

    target = right_side[0, 0]
    (rounded,) = solve((0,), target, inverse_pair, ())
    plan = make_plan(place, parent.reshape(1, 128), tile_pattern)
    before = ()
    for step in range(6):
        pieces = gather_panels(rounded, plan if step == 0 else None)
        parts = tile_products(step, plan, tile_scales, place, pieces, tiles, before)
        before = tuple(parts[4:])
        sums = (parts[0], *across_rows(parts[1:4]))
        if step == 2:
            rounded, forward = solve((0, 1), target, inverse_pair, sums, keep=True)
            target = forward
        elif step == 5:
            (solved,) = solve((1,), target, inverse_pair, sums, keep=True, send=False)
        else:
            (rounded,) = solve((step // 3,), target, inverse_pair, sums)
    return (forward[None, None], solved[None, None])


def solution(mesh):
    in_specs = (
        P("prow", "pcol", None, None),
        P(None, "pcol", "prow", None, None),
        P(None, "pcol", "prow"),
        P(None, "pcol", "prow"),
        P(),
        P(None, "prow", "pcol", None, None),
    )
    out_specs = (P("prow", "pcol", None, None), P("prow", "pcol", None, None))
    return jax.shard_map(shards, mesh=mesh, in_specs=in_specs, out_specs=out_specs, check_vma=False)
```

```python
import functools
import jax
import jax.numpy as jnp
from jax import lax
from jax.experimental import pallas as pl
from jax.experimental.pallas import tpu as pltpu
from jax.sharding import PartitionSpec as P

DEPTH = 4
B = 256
R = 128
SLOTS = 8
NEAR = ((0, 3, 1, 2), (0, 1, 2, 3))
FAR = ((0, 1, 3, 2), (0, 1, 3, 2))
ACROSS = ((0, 2, 1, 3), (0, 2, 1, 3))
ANY = pl.BlockSpec(memory_space=pl.ANY)
SMEM = pl.BlockSpec(memory_space=pltpu.SMEM)
VMEM = pl.BlockSpec(memory_space=pltpu.VMEM)
HBM = pl.BlockSpec(memory_space=pltpu.HBM)
LIMIT = 50 * 2**20


def near_pairs(n):
    return [(i, shifted(i, NEAR[i & 1][n], 1 if i & 1 == 0 else 3)) for i in range(32)]


def far_pairs(n):
    return [(i, shifted(i, FAR[i & 1][n], 3 if i & 1 == 0 else 1)) for i in range(32)]


def shifted(i, k, bit):
    return (i & ~(3 << bit)) | ((((i >> bit) + k) & 3) << bit)


def across_pairs(n):
    return [(i, (i + 32 * ACROSS[i & 1][n]) & 127) for i in range(128)]


def order_at(order, odd, shift):
    places = [sum(jnp.where(shift == k, n, 0) for n, k in enumerate(one)) for one in order]
    return jnp.where(odd, places[1], places[0])


CORE_PAIRS = [(i, i ^ 1) for i in range(32)]


def plan_kernel(place, parent, pattern, out):
    prow_at, pcol_at = place[0], place[1]
    down = lax.broadcasted_iota(jnp.int32, (128, 128), 0)
    across = lax.broadcasted_iota(jnp.int32, (128, 128), 1)

    def column(row):
        return jnp.broadcast_to(row, (128, 128)).T

    def total(values):
        return jnp.sum(values, axis=0, keepdims=True)

    matches = parent[...] == down
    depths = jnp.zeros((1, 128), jnp.int32)
    for repeat in range(DEPTH - 1):
        depths = total(jnp.where(matches, column(depths) + 1, 0))
    depth_column = column(depths)
    row_depth = total(jnp.where(down == (across & 96) + pcol_at, depth_column, 0))
    col_depth = total(jnp.where(down == (across & 31) + prow_at * 32, depth_column, 0))
    spread = (lax.broadcasted_iota(jnp.int32, (32, 128), 1) & 31) == lax.broadcasted_iota(jnp.int32, (32, 128), 0)
    kept = jnp.zeros((1, 128), jnp.float32)
    for row in range(4):
        ones = (jnp.broadcast_to(pattern[row], (8, 32)) == 1).astype(jnp.float32)
        wide = jnp.dot(ones, spread.astype(jnp.float32), preferred_element_type=jnp.float32)[:1]
        kept = jnp.where(across[:1] >> 5 == row, wide, kept)
    step = jnp.where(col_depth > row_depth, 3 - col_depth, jnp.where(col_depth < row_depth, 3 + col_depth, 6))
    step = jnp.where(kept > 0.5, step, 6)
    steps = column(step)
    before = (steps < step) | ((steps == step) & (down < across))
    places = total(before.astype(jnp.int32))
    out[0:1] = total(jnp.where(column(places) == across, down, 0))
    out[1:2] = total((steps < across).astype(jnp.int32))


def make_plan(place, parent, pattern):
    return pl.pallas_call(
        plan_kernel,
        out_shape=jax.ShapeDtypeStruct((2, 128), jnp.int32),
        in_specs=[SMEM, VMEM, VMEM],
        out_specs=VMEM,
        compiler_params=pltpu.CompilerParams(vmem_limit_bytes=LIMIT),
        cost_estimate=pl.CostEstimate(flops=2**22, bytes_accessed=2**12, transcendentals=0),
        name="make_plan",
    )(place, parent, pattern)


def fetch(sources, buffers, sems):
    fetched = [pltpu.make_async_copy(src, buf, sems.at[n]) for n, (src, buf) in enumerate(zip(sources, buffers))]
    for copy in fetched:
        copy.start()
    return fetched


def panel_place(pcol_at, col):
    x_back = ((pcol_at >> 3) - (col >> 3)) & 3
    y_back = ((pcol_at >> 1) - (col >> 1)) & 3
    far = jnp.where((col & 1) == 0, x_back, y_back)
    near = jnp.where((col & 1) == 0, y_back, x_back)
    odd = (col & 1) == 1
    return (col ^ pcol_at) & 1, order_at(FAR, odd, far), order_at(NEAR, odd, near)


def start_panel(pieces, pcol_at, col, buffer, sem):
    other, far, near_slot = panel_place(pcol_at, col)
    for e in range(2):
        for k in range(4):
            @pl.when((other == e) & (far == k))
            def _():
                pltpu.make_async_copy(pieces[e * 4 + k].at[near_slot], buffer, sem).start()


def tile_kernel(step, plan, scales, place, *refs):
    pieces, tiles, refs = refs[:8], refs[8], refs[9:]
    before, refs = (refs[0], refs[1:]) if step % 3 > 0 else (None, refs)
    outs, refs = refs[:4], refs[4:]
    after, refs = (refs[0], refs[1:]) if step % 3 < 2 else (None, refs)
    acc, tile_buf, panel_buf, tile_sem, panel_sem, before_sem = refs
    first, last = plan[1, step], plan[1, step + 1]
    prow_at, pcol_at = place[0], place[1]

    def start(n, slot):
        code = plan[0, n]
        row, col = code >> 5, code & 31

        pltpu.make_async_copy(tiles.at[row, col], tile_buf.at[slot], tile_sem.at[slot]).start()
        start_panel(pieces, pcol_at, col, panel_buf.at[slot], panel_sem.at[slot])

    if step % 3 > 0:
        previous = pltpu.make_async_copy(before, acc, before_sem)
        previous.start()
    def begin(n, carry):
        start(n, n - first)
        return carry

    lax.fori_loop(first, jnp.minimum(last, first + SLOTS), begin, 0)

    if step % 3 > 0:
        previous.wait()
    else:
        acc[...] = jnp.zeros_like(acc)

    def body(n, carry):
        slot = (n - first) % SLOTS
        code = plan[0, n]
        pltpu.make_async_copy(tiles.at[0, 0], tile_buf.at[slot], tile_sem.at[slot]).wait()
        pltpu.make_async_copy(pieces[0].at[0], panel_buf.at[slot], panel_sem.at[slot]).wait()
        product = jnp.dot(tile_buf[slot], panel_buf[slot], preferred_element_type=jnp.float32)
        row = code >> 5
        acc[row] = acc[row] + scales[row, 0, code & 31] * product

        @pl.when(n + SLOTS < last)
        def _():
            start(n + SLOTS, slot)
        return carry

    lax.fori_loop(first, last, body, 0)
    if after is not None:
        after[...] = acc[...]
    outs[0][...] = acc[prow_at]
    for k in range(1, 4):
        outs[k][...] = acc[(prow_at + jnp.where((pcol_at & 1) == 0, ACROSS[0][k], ACROSS[1][k])) & 3].astype(jnp.bfloat16)


def tile_products(step, plan, scales, place, pieces, tiles, before):
    out_shape = [jax.ShapeDtypeStruct((B, R), jnp.float32)] + [jax.ShapeDtypeStruct((B, R), jnp.bfloat16)] * 3
    if step % 3 < 2:
        out_shape = out_shape + [jax.ShapeDtypeStruct((4, B, R), jnp.float32)]
    return pl.pallas_call(
        functools.partial(tile_kernel, step),
        out_shape=out_shape,
        in_specs=[SMEM] * 3 + [ANY] * (9 + len(before)),
        out_specs=[VMEM] * len(out_shape),
        scratch_shapes=[
            pltpu.VMEM((4, B, R), jnp.float32),
            pltpu.VMEM((SLOTS, B, B), jnp.bfloat16),
            pltpu.VMEM((SLOTS, B, R), jnp.bfloat16),
            pltpu.SemaphoreType.DMA((SLOTS,)),
            pltpu.SemaphoreType.DMA((SLOTS,)),
            pltpu.SemaphoreType.DMA,
        ],
        compiler_params=pltpu.CompilerParams(vmem_limit_bytes=LIMIT),
        cost_estimate=pl.CostEstimate(flops=2 * 4 * B * B * R, bytes_accessed=4 * (B * B + B * R) * 2, transcendentals=0),
        name="tile_products",
    )(plan, scales, place, *pieces, tiles, *before)


def split(vectors):
    high = vectors.astype(jnp.bfloat16)
    return high, (vectors - high.astype(jnp.float32)).astype(jnp.bfloat16)


def apply_split(inverse, high, low):
    return jnp.dot(inverse, high, preferred_element_type=jnp.float32) + jnp.dot(inverse, low, preferred_element_type=jnp.float32)


def solve_kernel(uses, summed, keep, send, target, inverses, *refs):
    sums, refs = refs[:summed], refs[summed:]
    rounded, refs = (refs[0], refs[1:]) if send else (None, refs)
    solved, refs = (refs[0], refs[1:]) if keep else (None, refs)
    buffers, inverse_buf, sems = refs[:-2], refs[-2], refs[-1]
    inverse_copies = fetch([inverses.at[n] for n in uses], [inverse_buf.at[n] for n in range(len(uses))], sems.at[pl.ds(5, 2)])
    for copy in fetch((target,) + sums, buffers, sems):
        copy.wait()
    value = buffers[0][...]
    if sums:
        received = buffers[2][...].astype(jnp.float32) + buffers[3][...].astype(jnp.float32) + buffers[4][...].astype(jnp.float32)
        value = value - (buffers[1][...] + received)
    for n, use in enumerate(uses):
        inverse_copies[n].wait()
        value = apply_split(inverse_buf[n], *split(value))
        if n == 0 and solved is not None:
            solved[...] = value
    if rounded is not None:
        rounded[...] = value.astype(jnp.bfloat16)


def solve(uses, target, inverses, sums, keep=False, send=True):
    out_shape = []
    if send:
        out_shape.append(jax.ShapeDtypeStruct((B, R), jnp.bfloat16))
    if keep:
        out_shape.append(jax.ShapeDtypeStruct((B, R), jnp.float32))
    buffers = [pltpu.VMEM((B, R), jnp.float32)]
    if sums:
        buffers = buffers + [pltpu.VMEM((B, R), jnp.float32)] + [pltpu.VMEM((B, R), jnp.bfloat16)] * 3
    return pl.pallas_call(
        functools.partial(solve_kernel, uses, len(sums), keep, send),
        out_shape=out_shape,
        in_specs=[ANY] * (2 + len(sums)),
        out_specs=[VMEM] * len(out_shape),
        scratch_shapes=buffers + [pltpu.VMEM((len(uses), B, B), jnp.bfloat16), pltpu.SemaphoreType.DMA((7,))],
        compiler_params=pltpu.CompilerParams(vmem_limit_bytes=LIMIT),
        cost_estimate=pl.CostEstimate(flops=4 * B * B * R, bytes_accessed=B * R * 20, transcendentals=0),
        name="solve",
    )(target, inverses, *sums)


def stack_kernel(plan, *refs):
    panels, out, sems = refs[:4], refs[4], refs[5]
    for copy in fetch(panels, [out.at[k] for k in range(4)], sems):
        copy.wait()


def stack_after(plan, panels):
    return pl.pallas_call(
        stack_kernel,
        out_shape=jax.ShapeDtypeStruct((4, B, R), jnp.bfloat16),
        in_specs=[ANY] * 5,
        out_specs=ANY,
        scratch_shapes=[pltpu.SemaphoreType.DMA((4,))],
        compiler_params=pltpu.CompilerParams(vmem_limit_bytes=LIMIT),
        name="stack_after",
    )(plan, *panels)


def gather_panels(panel, plan=None):
    near = [panel] + [lax.ppermute(panel, "pcol", near_pairs(n)) for n in (1, 2, 3)]
    near = jnp.stack(near) if plan is None else stack_after(plan, near)
    far = [near] + [lax.ppermute(near, "pcol", far_pairs(n)) for n in (1, 2, 3)]
    return far + [lax.ppermute(piece, "pcol", CORE_PAIRS) for piece in far]


def across_rows(values):
    return [lax.ppermute(value, ("prow", "pcol"), across_pairs(n + 1)) for n, value in enumerate(values)]


def shards(right_side, factor_tiles, tile_scales, tile_pattern, parent, inverses):
    place = jnp.stack([lax.axis_index("prow"), lax.axis_index("pcol")]).astype(jnp.int32)
    tiles = factor_tiles[:, 0]
    inverse_pair = inverses[:, 0, 0]

    target = right_side[0, 0]
    (rounded,) = solve((0,), target, inverse_pair, ())
    plan = make_plan(place, parent.reshape(1, 128), tile_pattern)
    before = ()
    for step in range(6):
        pieces = gather_panels(rounded, plan if step == 0 else None)
        parts = tile_products(step, plan, tile_scales, place, pieces, tiles, before)
        before = tuple(parts[4:])
        sums = (parts[0], *across_rows(parts[1:4]))
        if step == 2:
            rounded, forward = solve((0, 1), target, inverse_pair, sums, keep=True)
            target = forward
        elif step == 5:
            (solved,) = solve((1,), target, inverse_pair, sums, keep=True, send=False)
        else:
            (rounded,) = solve((step // 3,), target, inverse_pair, sums)
    return (forward[None, None], solved[None, None])


def solution(mesh):
    in_specs = (
        P("prow", "pcol", None, None),
        P(None, "pcol", "prow", None, None),
        P(None, "pcol", "prow"),
        P(None, "pcol", "prow"),
        P(),
        P(None, "prow", "pcol", None, None),
    )
    out_specs = (P("prow", "pcol", None, None), P("prow", "pcol", None, None))
    return jax.shard_map(shards, mesh=mesh, in_specs=in_specs, out_specs=out_specs, check_vma=False)
```
